32 devices in a mesh: tile: 16 (over z, x, core), split: 2 (over y).
Axes of the slice: x: 2, y: 2, z: 4, core: 2. Of those that a mesh axis runs over, the one named last changes fastest.
Arguments:
- noisy_image: bfloat16 [16, 45, 128, 128], P('tile', None, 'split'), may hold values from -60 to 60
- seam_codes: int32 [16, 4], replicated, may hold values from 0 to 3
- timestep: int32 [1], replicated, may hold values from 0 to 999
- time_weight: float32 [48, 192], replicated, may hold values from -0.875 to 0.875
- bias_upper: float32 [192, 48], replicated, may hold values from -0.875 to 0.875
- bias_lower: float32 [192, 96], replicated, may hold values from -0.875 to 0.875
- kernel_upper_first: bfloat16 [3, 3, 48, 45], replicated, may hold values from -0.3125 to 0.3125
- kernel_upper_second: bfloat16 [3, 3, 48, 48], replicated, may hold values from -0.3125 to 0.3125
- kernel_lower_first: bfloat16 [3, 3, 96, 48], replicated, may hold values from -0.3125 to 0.3125
- kernel_lower_second: bfloat16 [3, 3, 96, 96], replicated, may hold values from -0.21875 to 0.21875
- kernel_decode_first: bfloat16 [3, 3, 48, 144], replicated, may hold values from -0.15625 to 0.15625
- kernel_decode_second: bfloat16 [3, 3, 48, 48], replicated, may hold values from -0.3125 to 0.3125
- output_weight: bfloat16 [45, 48], replicated, may hold values from -0.875 to 0.875
- gains_upper: float32 [4, 48], replicated, may hold values from 0.25 to 1.75
- shifts_upper: float32 [4, 48], replicated, may hold values from -1 to 1
- gains_lower: float32 [2, 96], replicated, may hold values from 0.25 to 1.75
- shifts_lower: float32 [2, 96], replicated, may hold values from -1 to 1
Outputs:
- predicted_noise: bfloat16 [16, 45, 128, 128], P('tile', None, 'split')
The draws below stay inside these ranges and needn't reach their ends.
All inputs are finite; a program needn't handle non-finite values.
Results may differ from the reference program's by a relative error of at most 0.018.
Values may be sent and summed in bfloat16 or wider, within the bound.
A program may use at most 128 MiB of HBM per device.

```python
import math
import jax
import jax.numpy as jnp
from jax import lax

CHANNELS = 45
WIDTH_ONE = 48
WIDTH_TWO = 96
EMBED = 192
GROUPS = 8
ROW_TILES = 4
SIDE = 128
TILES = 16


def draw_noisy_image(key, part):
    first_key = jax.random.fold_in(jax.random.fold_in(key, 17), 0)
    places = jnp.arange(TILES, dtype=jnp.float32)
    tile_scale = 1.0 + 2.0 * places / max(TILES - 1, 1)
    shape = (TILES, CHANNELS, SIDE, SIDE)
    base = jnp.clip(jax.random.normal(first_key, shape, jnp.float32), -6.0, 6.0)
    return (base * tile_scale[:, None, None, None]).astype(jnp.bfloat16)


def plant(entries, stream_key, least, top_value):
    shape = entries.shape
    spot = [jax.random.randint(jax.random.fold_in(stream_key, axis), (), 0, shape[axis]) for axis in range(len(shape))]
    entries = entries.at[tuple(spot)].set(least)
    longest = shape.index(max(shape))
    spot[longest] = (spot[longest] + 1) % shape[longest]
    return entries.at[tuple(spot)].set(top_value)


def normal_values(own_key, shape, scale, bound, kind=jnp.bfloat16):
    result = jax.random.normal(own_key, shape, jnp.float32) * scale
    return jnp.minimum(jnp.maximum(result, -bound), bound).astype(kind)


def setup_inputs(seed: int = 0) -> dict:
    key_list = jax.random.split(jax.random.key(seed), 18)
    noisy_image = draw_noisy_image(jax.random.fold_in(key_list[17], 71), 0)
    seam_codes = plant(jax.random.randint(key_list[1], (TILES, 4), 0, 4), jax.random.fold_in(key_list[1], 1), 0, 3).astype(jnp.int32)
    timestep = jax.random.randint(key_list[2], (1,), 0, 1000).astype(jnp.int32)
    time_weight = normal_values(key_list[3], (WIDTH_ONE, EMBED), WIDTH_ONE ** -0.5, 0.875, jnp.float32)
    bias_upper = normal_values(key_list[4], (EMBED, WIDTH_ONE), (EMBED // 4) ** -0.5, 0.875, jnp.float32)
    bias_lower = normal_values(key_list[5], (EMBED, WIDTH_TWO), (EMBED // 4) ** -0.5, 0.875, jnp.float32)
    kernel_upper_first = normal_values(key_list[6], (3, 3, WIDTH_ONE, CHANNELS), (9 * CHANNELS) ** -0.5, 0.3125)
    kernel_upper_second = normal_values(key_list[7], (3, 3, WIDTH_ONE, WIDTH_ONE), (9 * WIDTH_ONE) ** -0.5, 0.3125)
    kernel_lower_first = normal_values(key_list[8], (3, 3, WIDTH_TWO, WIDTH_ONE), (9 * WIDTH_ONE) ** -0.5, 0.3125)
    kernel_lower_second = normal_values(key_list[9], (3, 3, WIDTH_TWO, WIDTH_TWO), (9 * WIDTH_TWO) ** -0.5, 0.21875)
    kernel_decode_first = normal_values(key_list[10], (3, 3, WIDTH_ONE, WIDTH_TWO + WIDTH_ONE), (9 * (WIDTH_TWO + WIDTH_ONE)) ** -0.5, 0.15625)
    kernel_decode_second = normal_values(key_list[11], (3, 3, WIDTH_ONE, WIDTH_ONE), (9 * WIDTH_ONE) ** -0.5, 0.3125)
    output_weight = normal_values(key_list[12], (CHANNELS, WIDTH_ONE), WIDTH_ONE ** -0.5, 0.875)
    gains_upper = jnp.clip(1.0 + 0.15 * jax.random.normal(key_list[13], (4, WIDTH_ONE), jnp.float32), 0.25, 1.75)
    shifts_upper = normal_values(key_list[14], (4, WIDTH_ONE), 0.3, 1.0, jnp.float32)
    gains_lower = jnp.clip(1.0 + 0.15 * jax.random.normal(key_list[15], (2, WIDTH_TWO), jnp.float32), 0.25, 1.75)
    shifts_lower = normal_values(key_list[16], (2, WIDTH_TWO), 0.3, 1.0, jnp.float32)
    return {"noisy_image": noisy_image, "seam_codes": seam_codes, "timestep": timestep, "time_weight": time_weight, "bias_upper": bias_upper, "bias_lower": bias_lower, "kernel_upper_first": kernel_upper_first, "kernel_upper_second": kernel_upper_second, "kernel_lower_first": kernel_lower_first, "kernel_lower_second": kernel_lower_second, "kernel_decode_first": kernel_decode_first, "kernel_decode_second": kernel_decode_second, "output_weight": output_weight, "gains_upper": gains_upper, "shifts_upper": shifts_upper, "gains_lower": gains_lower, "shifts_lower": shifts_lower}


EPSILON = 1e-05

def side_strips(values):
    return jnp.stack([values[:, :, 0, ::-1], values[:, :, ::-1, -1], values[:, :, -1, :], values[:, :, :, 0]], axis=1)

def frame(block_values, upper, lower, west_column, east_column):
    stacked = jnp.concatenate([upper[:, None, :], block_values, lower[:, None, :]], axis=1)
    return jnp.concatenate([west_column[:, :, None], stacked, east_column[:, :, None]], axis=2)

def apply_taps(padded, kernel, height, width):
    channels = padded.shape[0]
    total = jnp.zeros((kernel.shape[2], height * width), jnp.float32)
    for row_off in range(3):
        for col_off in range(3):
            window = padded[:, row_off:row_off + height, col_off:col_off + width].reshape(channels, height * width)
            total = total + jnp.dot(kernel[row_off, col_off], window, preferred_element_type=jnp.float32)
    return total.reshape(kernel.shape[2], height, width)

def convolve(values, seam_codes, kernel):
    tile_count = values.shape[0]
    side_length = values.shape[2]
    edges = side_strips(values)
    offsets = (-ROW_TILES, 1, ROW_TILES, -1)

    def one_tile(place):
        block_values = lax.dynamic_index_in_dim(values, place, 0, False)
        code_row = lax.dynamic_index_in_dim(seam_codes, place, 0, False)
        strip_list = []
        for side_index in range(4):
            neighbour = (place + offsets[side_index]) % tile_count
            facing = (side_index + 2 + code_row[side_index]) % 4
            their_edges = lax.dynamic_index_in_dim(edges, neighbour, 0, False)
            strip_list.append(lax.dynamic_index_in_dim(their_edges, facing, 0, False))
        west_column = jnp.pad(strip_list[3][:, ::-1], ((0, 0), (1, 1)))
        east_column = jnp.pad(strip_list[1], ((0, 0), (1, 1)))
        padded = frame(block_values, strip_list[0], strip_list[2][:, ::-1], west_column, east_column)
        return apply_taps(padded, kernel, side_length, side_length)
    return lax.map(one_tile, jnp.arange(tile_count, dtype=jnp.int32))

def norm_act(values, gain, shift):
    tile_count, channels, height, width = values.shape
    grouped = values.reshape(tile_count, GROUPS, channels // GROUPS, height, width)
    mean = lax.optimization_barrier(jnp.mean(grouped, axis=(0, 2, 3, 4), keepdims=True))
    spread = lax.optimization_barrier(jnp.mean(jnp.square(grouped - mean), axis=(0, 2, 3, 4), keepdims=True))
    normed = ((grouped - mean) / jnp.sqrt(spread + EPSILON)).reshape(values.shape)
    scaled = normed * gain[None, :, None, None] + shift[None, :, None, None]
    return jax.nn.silu(scaled).astype(jnp.bfloat16)

def embedding(timestep, time_weight, bias_upper, bias_lower):
    moment = timestep[0].astype(jnp.float32)
    half_width = time_weight.shape[0] // 2
    frequencies = jnp.exp(-math.log(10000.0) * jnp.arange(half_width, dtype=jnp.float32) / half_width)
    angles = moment * frequencies
    features = jnp.concatenate([jnp.sin(angles), jnp.cos(angles)])[None, :]
    embedded = jax.nn.silu(jnp.dot(features, time_weight, precision=lax.Precision.HIGHEST, preferred_element_type=jnp.float32))
    first_bias = jnp.dot(embedded, bias_upper, precision=lax.Precision.HIGHEST, preferred_element_type=jnp.float32)[0]
    second_bias = jnp.dot(embedded, bias_lower, precision=lax.Precision.HIGHEST, preferred_element_type=jnp.float32)[0]
    return (first_bias, second_bias)

def reference(noisy_image, seam_codes, timestep, time_weight, bias_upper, bias_lower, kernel_upper_first, kernel_upper_second, kernel_lower_first, kernel_lower_second, kernel_decode_first, kernel_decode_second, output_weight, gains_upper, shifts_upper, gains_lower, shifts_lower):
    first_bias, second_bias = embedding(timestep, time_weight, bias_upper, bias_lower)
    first = norm_act(convolve(noisy_image, seam_codes, kernel_upper_first) + first_bias[None, :, None, None], gains_upper[0], shifts_upper[0])
    skip = norm_act(convolve(first, seam_codes, kernel_upper_second), gains_upper[1], shifts_upper[1])
    tile_count, width_one, side_length, _ = skip.shape
    half_side = side_length // 2
    pooled = lax.optimization_barrier(jnp.mean(skip.astype(jnp.float32).reshape(tile_count, width_one, half_side, 2, half_side, 2), axis=(3, 5))).astype(jnp.bfloat16)
    middle = norm_act(convolve(pooled, seam_codes, kernel_lower_first) + second_bias[None, :, None, None], gains_lower[0], shifts_lower[0])
    deep = norm_act(convolve(middle, seam_codes, kernel_lower_second), gains_lower[1], shifts_lower[1])
    widened = jnp.repeat(jnp.repeat(deep, 2, axis=2), 2, axis=3)
    joined = jnp.concatenate([widened, skip], axis=1)
    decoded = norm_act(convolve(joined, seam_codes, kernel_decode_first), gains_upper[2], shifts_upper[2])
    refined = norm_act(convolve(decoded, seam_codes, kernel_decode_second), gains_upper[3], shifts_upper[3])

    def project(place):
        block_values = lax.dynamic_index_in_dim(refined, place, 0, False)
        flat = jnp.dot(output_weight, block_values.reshape(width_one, side_length * side_length), preferred_element_type=jnp.float32)
        return flat.reshape(output_weight.shape[0], side_length, side_length).astype(jnp.bfloat16)
    return lax.map(project, jnp.arange(tile_count, dtype=jnp.int32))
```

```python
import functools
import math

import jax
import jax.numpy as jnp
from jax import lax
from jax.experimental import pallas as pl
from jax.experimental.pallas import tpu as pltpu
from jax.sharding import PartitionSpec as P

GROUPS = 8
ROW_TILES = 4
EPSILON = 1e-05
LANES = 128
MESH = pl.DeviceIdType.MESH
F32 = jnp.float32
BF16 = jnp.bfloat16
HIGH = lax.Precision.HIGHEST


def lanes_of(channels):
    return lax.broadcasted_iota(jnp.int32, (channels, LANES), 1)


def kernel(
    tiles, one, two, rows, cols, outputs,
    codes, image, params, w_uf, w_us, w_lf, w_ls, w_df, w_ds, w_out,
    out,
    x_one, x_low, x_mid, x_join, raw_up, raw_low, pool_ref, stats, stats_in, stats_two, stats_two_in, *rest,
):
    sends, recvs, inners = rest[0:7], rest[7:14], rest[14:21]
    send_sem, recv_sem, stat_send, stat_recv = rest[21:25]
    t, s = lax.axis_index("tile"), lax.axis_index("split")
    a, b = lax.div(t, ROW_TILES), lax.rem(t, ROW_TILES)
    depth = tiles // ROW_TILES
    plane = 2 * ROW_TILES
    half_rows, half_cols = rows // 2, cols // 2

    def across(offset):
        return lax.rem(t + offset + tiles, tiles)

    def plane_peer(step):
        place = lax.rem(b * 2 + s + step, plane)
        return (a * ROW_TILES + lax.div(place, 2), lax.rem(place, 2))

    def depth_peer(step):
        return (lax.rem(a + step, depth) * ROW_TILES + b, s)

    peers = [plane_peer(step) for step in range(1, plane)]
    peers += [depth_peer(step) for step in range(1, depth)]
    for offset in (ROW_TILES, -ROW_TILES, 1, -1):
        peers += [(across(offset), 0), (across(offset), 1)]
    barrier = pltpu.get_barrier_semaphore()
    for peer in peers:
        pl.semaphore_signal(barrier, inc=1, device_id=peer, device_id_type=MESH)
    pl.semaphore_wait(barrier, len(peers))

    def halo_copies(e):
        send, recv, inner = sends[e], recvs[e], inners[e]
        targets = [
            (0, (across(ROW_TILES), 0)), (0, (across(-ROW_TILES), 1)),
            (2, (across(-1), 0)), (2, (across(-1), 1)),
            (4, (across(1), 0)), (4, (across(1), 1)),
        ]
        copies = []
        for n, (slot, peer) in enumerate(targets):
            copies.append(pltpu.make_async_remote_copy(
                src_ref=send.at[pl.ds(0, 2)], dst_ref=recv.at[slot + s],
                send_sem=send_sem.at[e, n], recv_sem=recv_sem.at[e, slot + s],
                device_id=peer, device_id_type=MESH))
        copies.append(pltpu.make_async_remote_copy(
            src_ref=send.at[2], dst_ref=inner,
            send_sem=send_sem.at[e, 6], recv_sem=recv_sem.at[e, 6],
            device_id=(t, 1 - s), device_id_type=MESH))
        return copies

    def halo_start(e, top, bottom, columns):
        first = jnp.full(top.shape, s, jnp.int32) == 0
        sends[e][0] = jnp.where(first, top, bottom).astype(BF16)
        sends[e][1] = columns.astype(BF16)
        sends[e][2] = jnp.where(first, bottom, top).astype(BF16)
        for copy in halo_copies(e):
            copy.start()

    def halo_wait(e):
        send, recv, inner = sends[e], recvs[e], inners[e]
        for n in range(6):
            pltpu.make_async_remote_copy(
                src_ref=send.at[pl.ds(0, 2)], dst_ref=recv.at[n],
                send_sem=send_sem.at[e, n], recv_sem=recv_sem.at[e, n],
                device_id=(t, 1 - s), device_id_type=MESH).wait()
        pltpu.make_async_remote_copy(
            src_ref=send.at[2], dst_ref=inner,
            send_sem=send_sem.at[e, 6], recv_sem=recv_sem.at[e, 6],
            device_id=(t, 1 - s), device_id_type=MESH).wait()

    def mover(flip, off, wide, up):
        i = lax.broadcasted_iota(jnp.int32, (LANES, LANES), 0)
        p = lax.broadcasted_iota(jnp.int32, (LANES, LANES), 1) + off
        index = p + flip * (wide - 1 - 2 * p)
        if up:
            hit = (i * 2 == index) | (i * 2 + 1 == index)
        else:
            hit = i == index
        return jnp.where(hit & (p >= 0) & (p < wide), 1.0, 0.0).astype(BF16)

    def halo_finish(e, height, act, up):
        halo_wait(e)
        recv = recvs[e]
        channels = recv.shape[2]
        lane = lanes_of(channels)
        scale = 2 if up else 1
        tall, wide = height * scale, height * 2 * scale
        strips = []
        for place, side in ((0, 2 * s), (2, 1), (4, 3)):
            k = lax.rem(side + 2 + codes[t, side], 4)
            kv = jnp.full((channels, LANES), k, jnp.int32)
            zero, last = recv[place, 0].astype(F32), recv[place + 1, 0].astype(F32)
            col0, col1 = recv[place, 1].astype(F32), recv[place + 1, 1].astype(F32)
            upper_half = lane < height
            left = jnp.where(upper_half, col0, pltpu.roll(col1, height, 1))
            shift = (height - 64) % LANES
            right = jnp.where(
                upper_half, pltpu.roll(col0, 64, 1), pltpu.roll(col1, shift, 1) if shift else col1)
            cand = jnp.where(kv == 0, zero, jnp.where(kv == 1, right, jnp.where(kv == 2, last, left)))
            reverse = 1 if place == 4 else (s if place == 0 else 0)
            front = jnp.where(k < 2, 1, 0)
            flip = front + reverse - 2 * front * reverse
            off = 0 if place == 0 else s * tall - 1
            strips.append(jnp.dot(act(cand).astype(BF16), mover(flip, off, wide, up),
                                  preferred_element_type=F32))
        inner = act(inners[e][...].astype(F32)).astype(BF16)
        if up:
            inner = jnp.dot(inner, mover(0, 0, wide, True), preferred_element_type=F32)
        else:
            inner = inner.astype(F32)
        first = jnp.full((channels, LANES), s, jnp.int32) == 0
        upper = jnp.where(first, strips[0], inner)
        lower = jnp.where(first, inner, strips[0])
        return upper, lower, strips[2], strips[1]

    def put(ref, where_rows, j, y, west, east, wide, base, stride):
        channels = y.shape[0]
        lane = lanes_of(channels)
        left = jnp.where(lane == 0, pltpu.roll(west, lax.rem(LANES - j, LANES), 1), pltpu.roll(y, 1, 1))
        right = jnp.where(lane == wide - 1, pltpu.roll(east, wide - 1 - j, 1), pltpu.roll(y, LANES - 1, 1))
        left, mid, right = left.astype(BF16), y.astype(BF16), right.astype(BF16)
        for row in where_rows:
            ref[row, pl.ds(base, channels), :] = left
            ref[row, pl.ds(stride + base, channels), :] = mid
            ref[row, pl.ds(2 * stride + base, channels), :] = right

    def columns_with(columns, o, h, wide):
        lane = lanes_of(o.shape[0])
        columns = jnp.where(lane == h, pltpu.roll(o, h, 1), columns)
        return jnp.where(lane == 64 + h, pltpu.roll(o, lax.rem(64 + h + LANES - wide + 1, LANES), 1), columns)

    def conv(x_ref, w_ref, raw, height, wide, bias):
        outs = w_ref.shape[0]
        taps = 3 * x_ref.shape[1]

        def body(i, carry):
            acc, acc2, columns = carry
            for pair in range(2):
                h = i * 4 + pair * 2
                x = jnp.concatenate(
                    [x_ref[pl.ds(h, 3)].reshape(taps, LANES), x_ref[pl.ds(h + 1, 3)].reshape(taps, LANES)], axis=1)
                o = jnp.dot(w_ref[...], x, preferred_element_type=F32)
                for n in range(2):
                    part = o[:, n * LANES:(n + 1) * LANES]
                    if bias is not None:
                        part = part + bias
                    raw[h + n] = part
                    acc = acc + part
                    acc2 = acc2 + part * part
                    columns = columns_with(columns, part, h + n, wide)
            return acc, acc2, columns

        zero = jnp.zeros((outs, LANES), F32)
        return lax.fori_loop(0, height // 4, body, (zero, zero, zero))

    def reduce_stats(e, acc, acc2, height, wide, gain, shift):
        channels = acc.shape[0]
        size = channels // GROUPS
        g = lax.broadcasted_iota(jnp.int32, (GROUPS, channels), 0)
        c = lax.broadcasted_iota(jnp.int32, (GROUPS, channels), 1)
        member = jnp.where((c >= g * size) & (c < g * size + size), 1.0, 0.0).astype(F32)
        gt = lax.broadcasted_iota(jnp.int32, (channels, GROUPS), 1)
        ct = lax.broadcasted_iota(jnp.int32, (channels, GROUPS), 0)
        spread_out = jnp.where((ct >= gt * size) & (ct < gt * size + size), 1.0, 0.0).astype(F32)
        stats[e, pl.ds(0, GROUPS)] = jnp.dot(member, acc, precision=HIGH, preferred_element_type=F32)
        stats[e, pl.ds(GROUPS, GROUPS)] = jnp.dot(member, acc2, precision=HIGH, preferred_element_type=F32)
        copies = []
        for step in range(1, plane):
            copies.append(pltpu.make_async_remote_copy(
                src_ref=stats.at[e], dst_ref=stats_in.at[e, step],
                send_sem=stat_send.at[e, step], recv_sem=stat_recv.at[e, step],
                device_id=plane_peer(step), device_id_type=MESH))
        for copy in copies:
            copy.start()
        total = stats[e]
        for step, copy in enumerate(copies):
            copy.wait()
            total = total + stats_in[e, step + 1]
        stats_two[e] = total
        copies = []
        for step in range(1, depth):
            copies.append(pltpu.make_async_remote_copy(
                src_ref=stats_two.at[e], dst_ref=stats_two_in.at[e, step],
                send_sem=stat_send.at[e, plane + step], recv_sem=stat_recv.at[e, plane + step],
                device_id=depth_peer(step), device_id_type=MESH))
        for copy in copies:
            copy.start()
        for step, copy in enumerate(copies):
            copy.wait()
            total = total + stats_two_in[e, step + 1]
        total = jnp.where(lanes_of(2 * GROUPS) < wide, total, 0.0)
        means = jnp.sum(total, axis=1, keepdims=True) * (1.0 / (height * wide * size * 2 * tiles))
        mean = means[:GROUPS]
        inverse = lax.rsqrt(means[GROUPS:] - mean * mean + EPSILON)
        mean = jnp.broadcast_to(mean, (GROUPS, LANES))
        inverse = jnp.broadcast_to(inverse, (GROUPS, LANES))
        mean = jnp.dot(spread_out, mean, precision=HIGH, preferred_element_type=F32)
        inverse = jnp.dot(spread_out, inverse, precision=HIGH, preferred_element_type=F32)
        slope = 0.5 * gain * inverse
        offset = 0.5 * shift - mean * slope

        def act(u):
            y = u * slope + offset
            return y + y * jnp.tanh(y)
        return act

    def column(index, channels):
        return jnp.broadcast_to(params[pl.ds(0, channels), pl.ds(index, 1)], (channels, LANES))

    def same(value):
        return value

    def fill_edges(ref, height, wide, edges, base, stride):
        upper, lower, west, east = edges
        put(ref, [0], 0, upper, west, east, wide, base, stride)
        put(ref, [height + 1], height + 1, lower, west, east, wide, base, stride)

    def image_columns(h, columns):
        return columns_with(columns, image[h].astype(F32), h, cols)

    columns = lax.fori_loop(0, rows, image_columns, jnp.zeros((one, LANES), F32))
    halo_start(0, image[0].astype(F32), image[rows - 1].astype(F32), columns)
    edges = halo_finish(0, rows, same, False)
    fill_edges(x_one, rows, cols, edges, 0, one)

    def fill_image(h, c):
        put(x_one, [h + 1], h + 1, image[h].astype(F32), edges[2], edges[3], cols, 0, one)
        return c
    lax.fori_loop(0, rows, fill_image, 0)

    acc, acc2, columns = conv(x_one, w_uf, raw_up, rows, cols, column(12, one))
    halo_start(1, raw_up[0], raw_up[rows - 1], columns)
    act = reduce_stats(0, acc, acc2, rows, cols, column(0, one), column(4, one))
    edges = halo_finish(1, rows, act, False)
    fill_edges(x_one, rows, cols, edges, 0, one)

    def fill_first(h, c):
        put(x_one, [h + 1], h + 1, act(raw_up[h]), edges[2], edges[3], cols, 0, one)
        return c
    lax.fori_loop(0, rows, fill_first, 0)

    acc, acc2, columns = conv(x_one, w_us, raw_up, rows, cols, None)
    halo_start(2, raw_up[0], raw_up[rows - 1], columns)
    act_skip = reduce_stats(1, acc, acc2, rows, cols, column(1, one), column(5, one))
    skip_edges = halo_finish(2, rows, act_skip, False)
    fill_edges(x_join, rows, cols, skip_edges, two, one + two)
    i = lax.broadcasted_iota(jnp.int32, (LANES, LANES), 0)
    j = lax.broadcasted_iota(jnp.int32, (LANES, LANES), 1)
    pooling = jnp.where((i == 2 * j) | (i == 2 * j + 1), 0.25, 0.0).astype(BF16)

    def fill_skip(h, columns):
        pooled = jnp.zeros((one, LANES), F32)
        for n in range(2):
            y = act_skip(raw_up[2 * h + n])
            put(x_join, [2 * h + n + 1], 2 * h + n + 1, y, skip_edges[2], skip_edges[3], cols, two, one + two)
            pooled = pooled + jnp.dot(y.astype(BF16), pooling, preferred_element_type=F32)
        pool_ref[h] = pooled
        return columns_with(columns, pooled, h, half_cols)
    columns = lax.fori_loop(0, half_rows, fill_skip, jnp.zeros((one, LANES), F32))
    halo_start(3, pool_ref[0], pool_ref[half_rows - 1], columns)
    edges = halo_finish(3, half_rows, same, False)
    fill_edges(x_low, half_rows, half_cols, edges, 0, one)

    def fill_pooled(h, c):
        put(x_low, [h + 1], h + 1, pool_ref[h], edges[2], edges[3], half_cols, 0, one)
        return c
    lax.fori_loop(0, half_rows, fill_pooled, 0)

    acc, acc2, columns = conv(x_low, w_lf, raw_low, half_rows, half_cols, column(13, two))
    halo_start(4, raw_low[0], raw_low[half_rows - 1], columns)
    act = reduce_stats(2, acc, acc2, half_rows, half_cols, column(8, two), column(10, two))
    edges = halo_finish(4, half_rows, act, False)
    fill_edges(x_mid, half_rows, half_cols, edges, 0, two)

    def fill_middle(h, c):
        put(x_mid, [h + 1], h + 1, act(raw_low[h]), edges[2], edges[3], half_cols, 0, two)
        return c
    lax.fori_loop(0, half_rows, fill_middle, 0)

    acc, acc2, columns = conv(x_mid, w_ls, raw_low, half_rows, half_cols, None)
    halo_start(5, raw_low[0], raw_low[half_rows - 1], columns)
    act_deep = reduce_stats(3, acc, acc2, half_rows, half_cols, column(9, two), column(11, two))
    deep_edges = halo_finish(5, half_rows, act_deep, True)
    fill_edges(x_join, rows, cols, deep_edges, 0, one + two)
    widen = mover(0, 0, cols, True)

    def fill_deep(h, c):
        y = jnp.dot(act_deep(raw_low[h]).astype(BF16), widen, preferred_element_type=F32)
        put(x_join, [2 * h + 1, 2 * h + 2], 2 * h + 1, y, deep_edges[2], deep_edges[3], cols, 0, one + two)
        return c
    lax.fori_loop(0, half_rows, fill_deep, 0)

    acc, acc2, columns = conv(x_join, w_df, raw_up, rows, cols, None)
    halo_start(6, raw_up[0], raw_up[rows - 1], columns)
    act_dec = reduce_stats(4, acc, acc2, rows, cols, column(2, one), column(6, one))
    dec_edges = halo_finish(6, rows, act_dec, False)
    fill_edges(x_one, rows, cols, dec_edges, 0, one)

    def fill_decoded(h, c):
        put(x_one, [h + 1], h + 1, act_dec(raw_up[h]), dec_edges[2], dec_edges[3], cols, 0, one)
        return c
    lax.fori_loop(0, rows, fill_decoded, 0)

    acc, acc2, columns = conv(x_one, w_ds, raw_up, rows, cols, None)
    act_ref = reduce_stats(5, acc, acc2, rows, cols, column(3, one), column(7, one))

    def project(h, c):
        y = jnp.concatenate([act_ref(raw_up[2 * h]), act_ref(raw_up[2 * h + 1])], axis=1).astype(BF16)
        o = jnp.dot(w_out[...], y, preferred_element_type=F32).astype(BF16)
        out[2 * h] = o[:, :LANES]
        out[2 * h + 1] = o[:, LANES:]
        return c
    lax.fori_loop(0, half_rows, project, 0)


def embedding(timestep, time_weight, bias_upper, bias_lower):
    moment = timestep[0].astype(F32)
    half_width = time_weight.shape[0] // 2
    frequencies = jnp.exp(-math.log(10000.0) * jnp.arange(half_width, dtype=F32) / half_width)
    angles = moment * frequencies
    features = jnp.concatenate([jnp.sin(angles), jnp.cos(angles)])[None, :]
    embedded = jax.nn.silu(jnp.dot(features, time_weight, precision=HIGH, preferred_element_type=F32))
    both = jnp.concatenate([bias_upper, bias_lower], axis=1)
    biases = jnp.dot(embedded, both, precision=HIGH, preferred_element_type=F32)[0]
    return biases[: bias_upper.shape[1]], biases[bias_upper.shape[1]:]


def flat(weight, channels):
    pad = channels - weight.shape[3]
    if pad:
        weight = jnp.pad(weight, ((0, 0), (0, 0), (0, 0), (0, pad)))
    return jnp.transpose(weight, (2, 0, 1, 3)).reshape(weight.shape[2], -1)


def per_device(
    noisy_image, seam_codes, timestep, time_weight, bias_upper, bias_lower,
    kernel_upper_first, kernel_upper_second, kernel_lower_first, kernel_lower_second,
    kernel_decode_first, kernel_decode_second, output_weight,
    gains_upper, shifts_upper, gains_lower, shifts_lower,
):
    tiles = lax.axis_size("tile")
    _, channels, rows, cols = noisy_image.shape
    one, two = gains_upper.shape[1], gains_lower.shape[1]
    assert lax.axis_size("split") == 2 and cols == LANES and rows * 2 == cols
    first_bias, second_bias = embedding(timestep, time_weight, bias_upper, bias_lower)
    wide = lambda v: jnp.pad(v, ((0, 0), (0, two - v.shape[1])))
    params = jnp.concatenate(
        [wide(gains_upper), wide(shifts_upper), gains_lower, shifts_lower, wide(first_bias[None]),
         second_bias[None]], axis=0).T
    image = jnp.pad(jnp.transpose(noisy_image[0], (1, 0, 2)), ((0, 0), (0, one - channels), (0, 0)))
    projection = jnp.pad(output_weight, ((0, one - channels), (0, 0)))
    widths = (one, one, one, one, two, two, one)
    depth = tiles // ROW_TILES
    plane = 2 * ROW_TILES
    vmem = pl.BlockSpec(memory_space=pltpu.VMEM)
    result = pl.pallas_call(
        functools.partial(kernel, tiles, one, two, rows, cols, channels),
        out_shape=jax.ShapeDtypeStruct((rows, one, cols), BF16),
        in_specs=[pl.BlockSpec(memory_space=pltpu.SMEM)] + [vmem] * 9,
        out_specs=vmem,
        scratch_shapes=[
            pltpu.VMEM((rows + 2, 3 * one, LANES), BF16),
            pltpu.VMEM((rows // 2 + 2, 3 * one, LANES), BF16),
            pltpu.VMEM((rows // 2 + 2, 3 * two, LANES), BF16),
            pltpu.VMEM((rows + 2, 3 * (one + two), LANES), BF16),
            pltpu.VMEM((rows, one, LANES), F32),
            pltpu.VMEM((rows // 2, two, LANES), F32),
            pltpu.VMEM((rows // 2, one, LANES), F32),
            pltpu.VMEM((6, 2 * GROUPS, LANES), F32),
            pltpu.VMEM((6, plane, 2 * GROUPS, LANES), F32),
            pltpu.VMEM((6, 2 * GROUPS, LANES), F32),
            pltpu.VMEM((6, depth, 2 * GROUPS, LANES), F32),
        ]
        + [pltpu.VMEM((3, width, LANES), BF16) for width in widths]
        + [pltpu.VMEM((6, 2, width, LANES), BF16) for width in widths]
        + [pltpu.VMEM((width, LANES), BF16) for width in widths]
        + [
            pltpu.SemaphoreType.DMA((7, 7)),
            pltpu.SemaphoreType.DMA((7, 7)),
            pltpu.SemaphoreType.DMA((6, plane + depth)),
            pltpu.SemaphoreType.DMA((6, plane + depth)),
        ],
        compiler_params=pltpu.CompilerParams(
            collective_id=0, has_side_effects=True, vmem_limit_bytes=48 * 1024 * 1024),
    )(
        seam_codes, image, params,
        flat(kernel_upper_first, one), flat(kernel_upper_second, one),
        flat(kernel_lower_first, one), flat(kernel_lower_second, two),
        flat(kernel_decode_first, one + two), flat(kernel_decode_second, one), projection,
    )
    return jnp.transpose(result[:, :channels], (1, 0, 2))[None]


def solution(mesh):
    placed = (P("tile", None, "split", None),) + (P(),) * 16
    return jax.shard_map(
        per_device, mesh=mesh, in_specs=placed, out_specs=P("tile", None, "split", None), check_vma=False,
    )
```

```python
import functools
import math

import jax
import jax.numpy as jnp
from jax import lax
from jax.experimental import pallas as pl
from jax.experimental.pallas import tpu as pltpu
from jax.sharding import PartitionSpec as P

GROUPS = 8
ROW_TILES = 4
EPSILON = 1e-05
LANES = 128
MESH = pl.DeviceIdType.MESH
F32 = jnp.float32
BF16 = jnp.bfloat16
HIGH = lax.Precision.HIGHEST


def lanes_of(channels):
    return lax.broadcasted_iota(jnp.int32, (channels, LANES), 1)


def kernel(
    tiles, one, two, rows, cols, outputs,
    codes, image, params, w_uf, w_us, w_lf, w_ls, w_df, w_ds, w_out,
    out,
    x_one, x_low, x_mid, x_join, raw_up, raw_low, pool_ref, stats, *rest,
):
    sends, recvs, inners = rest[0:7], rest[7:14], rest[14:21]
    send_sem, recv_sem, stat_send, stat_recv = rest[21:25]
    t, s = lax.axis_index("tile"), lax.axis_index("split")
    devices = 2 * tiles
    half_rows, half_cols = rows // 2, cols // 2

    def across(offset):
        return lax.rem(t + offset + tiles, tiles)

    def peer_at(step):
        place = lax.rem(t * 2 + s + step, devices)
        return (lax.div(place, 2), lax.rem(place, 2))

    peers = [peer_at(step) for step in range(1, devices)]
    barrier = pltpu.get_barrier_semaphore()
    for peer in peers:
        pl.semaphore_signal(barrier, inc=1, device_id=peer, device_id_type=MESH)
    pl.semaphore_wait(barrier, len(peers))

    def halo_copies(e):
        send, recv, inner = sends[e], recvs[e], inners[e]
        targets = [
            (0, 0, (across(ROW_TILES), 0)), (1, 0, (across(-ROW_TILES), 1)),
            (2, 2, (across(-1), 0)), (2, 2, (across(-1), 1)),
            (3, 4, (across(1), 0)), (3, 4, (across(1), 1)),
        ]
        copies = []
        for n, (strip, slot, peer) in enumerate(targets):
            copies.append(pltpu.make_async_remote_copy(
                src_ref=send.at[strip], dst_ref=recv.at[slot + s],
                send_sem=send_sem.at[e, n], recv_sem=recv_sem.at[e, slot + s],
                device_id=peer, device_id_type=MESH))
        copies.append(pltpu.make_async_remote_copy(
            src_ref=send.at[4], dst_ref=inner,
            send_sem=send_sem.at[e, 6], recv_sem=recv_sem.at[e, 6],
            device_id=(t, 1 - s), device_id_type=MESH))
        return copies

    def facing(tile, side):
        return lax.rem(side + 2 + codes[tile, side], 4)

    def halo_start(e, top, bottom, columns):
        first = jnp.full(top.shape, s, jnp.int32) == 0
        outer = jnp.where(first, top, bottom)
        right = pltpu.roll(columns, 64, 1)
        for n, (offset, side) in enumerate(((ROW_TILES, 0), (-ROW_TILES, 2), (-1, 1), (1, 3))):
            kv = jnp.full(top.shape, facing(across(offset), side), jnp.int32)
            sends[e][n] = jnp.where(kv == 1, right, jnp.where(kv == 3, columns, outer)).astype(BF16)
        sends[e][4] = jnp.where(first, bottom, top).astype(BF16)
        for copy in halo_copies(e):
            copy.start()

    def halo_wait(e):
        send, recv, inner = sends[e], recvs[e], inners[e]
        for n in range(6):
            pltpu.make_async_remote_copy(
                src_ref=send.at[0], dst_ref=recv.at[n],
                send_sem=send_sem.at[e, n], recv_sem=recv_sem.at[e, n],
                device_id=(t, 1 - s), device_id_type=MESH).wait()
        pltpu.make_async_remote_copy(
            src_ref=send.at[4], dst_ref=inner,
            send_sem=send_sem.at[e, 6], recv_sem=recv_sem.at[e, 6],
            device_id=(t, 1 - s), device_id_type=MESH).wait()

    def mover(flip, off, wide, up):
        i = lax.broadcasted_iota(jnp.int32, (LANES, LANES), 0)
        p = lax.broadcasted_iota(jnp.int32, (LANES, LANES), 1) + off
        index = p + flip * (wide - 1 - 2 * p)
        if up:
            hit = (i * 2 == index) | (i * 2 + 1 == index)
        else:
            hit = i == index
        return jnp.where(hit & (p >= 0) & (p < wide), 1.0, 0.0).astype(BF16)

    def halo_finish(e, height, act, up):
        halo_wait(e)
        recv = recvs[e]
        channels = recv.shape[1]
        lane = lanes_of(channels)
        scale = 2 if up else 1
        tall, wide = height * scale, height * 2 * scale
        strips = []
        for place, side in ((0, 2 * s), (2, 1), (4, 3)):
            k = facing(t, side)
            kv = jnp.full((channels, LANES), k, jnp.int32)
            zero, last = recv[place].astype(F32), recv[place + 1].astype(F32)
            halves = jnp.where(lane < height, zero, pltpu.roll(last, height, 1))
            cand = jnp.where(kv == 0, zero, jnp.where(kv == 2, last, halves))
            reverse = 1 if place == 4 else (s if place == 0 else 0)
            front = jnp.where(k < 2, 1, 0)
            flip = front + reverse - 2 * front * reverse
            off = 0 if place == 0 else s * tall - 1
            strips.append(jnp.dot(act(cand).astype(BF16), mover(flip, off, wide, up),
                                  preferred_element_type=F32))
        inner = act(inners[e][...].astype(F32)).astype(BF16)
        if up:
            inner = jnp.dot(inner, mover(0, 0, wide, True), preferred_element_type=F32)
        else:
            inner = inner.astype(F32)
        first = jnp.full((channels, LANES), s, jnp.int32) == 0
        upper = jnp.where(first, strips[0], inner)
        lower = jnp.where(first, inner, strips[0])
        return upper, lower, strips[2], strips[1]

    def put(ref, where_rows, j, y, west, east, wide, base, stride):
        channels = y.shape[0]
        lane = lanes_of(channels)
        left = jnp.where(lane == 0, pltpu.roll(west, lax.rem(LANES - j, LANES), 1), pltpu.roll(y, 1, 1))
        right = jnp.where(lane == wide - 1, pltpu.roll(east, wide - 1 - j, 1), pltpu.roll(y, LANES - 1, 1))
        left, mid, right = left.astype(BF16), y.astype(BF16), right.astype(BF16)
        for row in where_rows:
            ref[row, pl.ds(base, channels), :] = left
            ref[row, pl.ds(stride + base, channels), :] = mid
            ref[row, pl.ds(2 * stride + base, channels), :] = right

    def columns_with(columns, o, h, wide):
        lane = lanes_of(o.shape[0])
        columns = jnp.where(lane == h, pltpu.roll(o, h, 1), columns)
        return jnp.where(lane == 64 + h, pltpu.roll(o, lax.rem(64 + h + LANES - wide + 1, LANES), 1), columns)

    def conv(x_ref, w_ref, raw, height, wide, bias):
        outs = w_ref.shape[0]
        taps = 3 * x_ref.shape[1]

        def body(i, carry):
            acc, acc2, columns = carry
            for pair in range(2):
                h = i * 4 + pair * 2
                x = jnp.concatenate(
                    [x_ref[pl.ds(h, 3)].reshape(taps, LANES), x_ref[pl.ds(h + 1, 3)].reshape(taps, LANES)], axis=1)
                o = jnp.dot(w_ref[...], x, preferred_element_type=F32)
                for n in range(2):
                    part = o[:, n * LANES:(n + 1) * LANES]
                    if bias is not None:
                        part = part + bias
                    raw[h + n] = part
                    acc = acc + part
                    acc2 = acc2 + part * part
                    columns = columns_with(columns, part, h + n, wide)
            return acc, acc2, columns

        zero = jnp.zeros((outs, LANES), F32)
        return lax.fori_loop(0, height // 4, body, (zero, zero, zero))

    def reduce_stats(e, acc, acc2, height, wide, gain, shift, meanwhile):
        channels = acc.shape[0]
        size = channels // GROUPS
        g = lax.broadcasted_iota(jnp.int32, (GROUPS, channels), 0)
        c = lax.broadcasted_iota(jnp.int32, (GROUPS, channels), 1)
        member = jnp.where((c >= g * size) & (c < g * size + size), 1.0, 0.0).astype(F32)
        gt = lax.broadcasted_iota(jnp.int32, (channels, GROUPS), 1)
        ct = lax.broadcasted_iota(jnp.int32, (channels, GROUPS), 0)
        spread_out = jnp.where((ct >= gt * size) & (ct < gt * size + size), 1.0, 0.0).astype(F32)
        stats[e, 0, pl.ds(0, GROUPS)] = jnp.dot(member, acc, precision=HIGH, preferred_element_type=F32)
        stats[e, 0, pl.ds(GROUPS, GROUPS)] = jnp.dot(member, acc2, precision=HIGH, preferred_element_type=F32)
        for step in range(1, devices):
            pltpu.make_async_remote_copy(
                src_ref=stats.at[e, 0], dst_ref=stats.at[e, step],
                send_sem=stat_send.at[e], recv_sem=stat_recv.at[e],
                device_id=peer_at(step), device_id_type=MESH).start()
        meanwhile()
        arrived = stats.at[e, pl.ds(1, devices - 1)]
        pltpu.make_async_remote_copy(
            src_ref=arrived, dst_ref=arrived, send_sem=stat_send.at[e], recv_sem=stat_recv.at[e],
            device_id=peer_at(1), device_id_type=MESH).wait()
        total = jnp.sum(stats[e], axis=0)
        total = jnp.where(lanes_of(2 * GROUPS) < wide, total, 0.0)
        means = jnp.sum(total, axis=1, keepdims=True) * (1.0 / (height * wide * size * 2 * tiles))
        mean = means[:GROUPS]
        inverse = lax.rsqrt(means[GROUPS:] - mean * mean + EPSILON)
        mean = jnp.broadcast_to(mean, (GROUPS, LANES))
        inverse = jnp.broadcast_to(inverse, (GROUPS, LANES))
        mean = jnp.dot(spread_out, mean, precision=HIGH, preferred_element_type=F32)
        inverse = jnp.dot(spread_out, inverse, precision=HIGH, preferred_element_type=F32)
        slope = 0.5 * gain * inverse
        offset = 0.5 * shift - mean * slope

        def act(u):
            y = u * slope + offset
            return y + y * jnp.tanh(y)
        return act

    def column(index, channels):
        return jnp.broadcast_to(params[pl.ds(0, channels), pl.ds(index, 1)], (channels, LANES))

    def same(value):
        return value

    def fill_edges(ref, height, wide, edges, base, stride):
        upper, lower, west, east = edges
        put(ref, [0], 0, upper, west, east, wide, base, stride)
        put(ref, [height + 1], height + 1, lower, west, east, wide, base, stride)

    def image_columns(h, columns):
        return columns_with(columns, image[h].astype(F32), h, cols)

    columns = lax.fori_loop(0, rows, image_columns, jnp.zeros((one, LANES), F32), unroll=8)
    halo_start(0, image[0].astype(F32), image[rows - 1].astype(F32), columns)
    edges = halo_finish(0, rows, same, False)
    fill_edges(x_one, rows, cols, edges, 0, one)

    def fill_image(h, c):
        put(x_one, [h + 1], h + 1, image[h].astype(F32), edges[2], edges[3], cols, 0, one)
        return c
    lax.fori_loop(0, rows, fill_image, 0, unroll=8)

    acc, acc2, columns = conv(x_one, w_uf, raw_up, rows, cols, column(12, one))
    act = reduce_stats(0, acc, acc2, rows, cols, column(0, one), column(4, one),
        lambda: halo_start(1, raw_up[0], raw_up[rows - 1], columns))
    edges = halo_finish(1, rows, act, False)
    fill_edges(x_one, rows, cols, edges, 0, one)

    def fill_first(h, c):
        put(x_one, [h + 1], h + 1, act(raw_up[h]), edges[2], edges[3], cols, 0, one)
        return c
    lax.fori_loop(0, rows, fill_first, 0, unroll=8)

    acc, acc2, columns = conv(x_one, w_us, raw_up, rows, cols, None)
    act_skip = reduce_stats(1, acc, acc2, rows, cols, column(1, one), column(5, one),
        lambda: halo_start(2, raw_up[0], raw_up[rows - 1], columns))
    skip_edges = halo_finish(2, rows, act_skip, False)
    fill_edges(x_join, rows, cols, skip_edges, two, one + two)
    i = lax.broadcasted_iota(jnp.int32, (LANES, LANES), 0)
    j = lax.broadcasted_iota(jnp.int32, (LANES, LANES), 1)
    pooling = jnp.where((i == 2 * j) | (i == 2 * j + 1), 0.25, 0.0).astype(BF16)

    def fill_skip(h, columns):
        pooled = jnp.zeros((one, LANES), F32)
        for n in range(2):
            y = act_skip(raw_up[2 * h + n])
            put(x_join, [2 * h + n + 1], 2 * h + n + 1, y, skip_edges[2], skip_edges[3], cols, two, one + two)
            pooled = pooled + jnp.dot(y.astype(BF16), pooling, preferred_element_type=F32)
        pool_ref[h] = pooled
        return columns_with(columns, pooled, h, half_cols)
    columns = lax.fori_loop(0, half_rows, fill_skip, jnp.zeros((one, LANES), F32), unroll=8)
    halo_start(3, pool_ref[0], pool_ref[half_rows - 1], columns)
    edges = halo_finish(3, half_rows, same, False)
    fill_edges(x_low, half_rows, half_cols, edges, 0, one)

    def fill_pooled(h, c):
        put(x_low, [h + 1], h + 1, pool_ref[h], edges[2], edges[3], half_cols, 0, one)
        return c
    lax.fori_loop(0, half_rows, fill_pooled, 0, unroll=8)

    acc, acc2, columns = conv(x_low, w_lf, raw_low, half_rows, half_cols, column(13, two))
    act = reduce_stats(2, acc, acc2, half_rows, half_cols, column(8, two), column(10, two),
        lambda: halo_start(4, raw_low[0], raw_low[half_rows - 1], columns))
    edges = halo_finish(4, half_rows, act, False)
    fill_edges(x_mid, half_rows, half_cols, edges, 0, two)

    def fill_middle(h, c):
        put(x_mid, [h + 1], h + 1, act(raw_low[h]), edges[2], edges[3], half_cols, 0, two)
        return c
    lax.fori_loop(0, half_rows, fill_middle, 0, unroll=8)

    acc, acc2, columns = conv(x_mid, w_ls, raw_low, half_rows, half_cols, None)
    act_deep = reduce_stats(3, acc, acc2, half_rows, half_cols, column(9, two), column(11, two),
        lambda: halo_start(5, raw_low[0], raw_low[half_rows - 1], columns))
    deep_edges = halo_finish(5, half_rows, act_deep, True)
    fill_edges(x_join, rows, cols, deep_edges, 0, one + two)
    widen = mover(0, 0, cols, True)

    def fill_deep(h, c):
        y = jnp.dot(act_deep(raw_low[h]).astype(BF16), widen, preferred_element_type=F32)
        put(x_join, [2 * h + 1, 2 * h + 2], 2 * h + 1, y, deep_edges[2], deep_edges[3], cols, 0, one + two)
        return c
    lax.fori_loop(0, half_rows, fill_deep, 0, unroll=8)

    acc, acc2, columns = conv(x_join, w_df, raw_up, rows, cols, None)
    act_dec = reduce_stats(4, acc, acc2, rows, cols, column(2, one), column(6, one),
        lambda: halo_start(6, raw_up[0], raw_up[rows - 1], columns))
    dec_edges = halo_finish(6, rows, act_dec, False)
    fill_edges(x_one, rows, cols, dec_edges, 0, one)

    def fill_decoded(h, c):
        put(x_one, [h + 1], h + 1, act_dec(raw_up[h]), dec_edges[2], dec_edges[3], cols, 0, one)
        return c
    lax.fori_loop(0, rows, fill_decoded, 0, unroll=8)

    acc, acc2, columns = conv(x_one, w_ds, raw_up, rows, cols, None)
    act_ref = reduce_stats(5, acc, acc2, rows, cols, column(3, one), column(7, one), lambda: None)

    def project(h, c):
        y = jnp.concatenate([act_ref(raw_up[2 * h]), act_ref(raw_up[2 * h + 1])], axis=1).astype(BF16)
        o = jnp.dot(w_out[...], y, preferred_element_type=F32).astype(BF16)
        out[2 * h] = o[:, :LANES]
        out[2 * h + 1] = o[:, LANES:]
        return c
    lax.fori_loop(0, half_rows, project, 0, unroll=8)


def embedding(timestep, time_weight, bias_upper, bias_lower):
    moment = timestep[0].astype(F32)
    half_width = time_weight.shape[0] // 2
    frequencies = jnp.exp(-math.log(10000.0) * jnp.arange(half_width, dtype=F32) / half_width)
    angles = moment * frequencies
    features = jnp.concatenate([jnp.sin(angles), jnp.cos(angles)])[None, :]
    embedded = jax.nn.silu(jnp.dot(features, time_weight, precision=HIGH, preferred_element_type=F32))
    both = jnp.concatenate([bias_upper, bias_lower], axis=1)
    biases = jnp.dot(embedded, both, precision=HIGH, preferred_element_type=F32)[0]
    return biases[: bias_upper.shape[1]], biases[bias_upper.shape[1]:]


def flat(weight, channels):
    pad = channels - weight.shape[3]
    if pad:
        weight = jnp.pad(weight, ((0, 0), (0, 0), (0, 0), (0, pad)))
    return jnp.transpose(weight, (2, 0, 1, 3)).reshape(weight.shape[2], -1)


def per_device(
    noisy_image, seam_codes, timestep, time_weight, bias_upper, bias_lower,
    kernel_upper_first, kernel_upper_second, kernel_lower_first, kernel_lower_second,
    kernel_decode_first, kernel_decode_second, output_weight,
    gains_upper, shifts_upper, gains_lower, shifts_lower,
):
    tiles = lax.axis_size("tile")
    _, channels, rows, cols = noisy_image.shape
    one, two = gains_upper.shape[1], gains_lower.shape[1]
    assert lax.axis_size("split") == 2 and cols == LANES and rows * 2 == cols
    first_bias, second_bias = embedding(timestep, time_weight, bias_upper, bias_lower)
    wide = lambda v: jnp.pad(v, ((0, 0), (0, two - v.shape[1])))
    params = jnp.concatenate(
        [wide(gains_upper), wide(shifts_upper), gains_lower, shifts_lower, wide(first_bias[None]),
         second_bias[None]], axis=0).T
    image = jnp.pad(jnp.transpose(noisy_image[0], (1, 0, 2)), ((0, 0), (0, one - channels), (0, 0)))
    projection = jnp.pad(output_weight, ((0, one - channels), (0, 0)))
    widths = (one, one, one, one, two, two, one)
    vmem = pl.BlockSpec(memory_space=pltpu.VMEM)
    result = pl.pallas_call(
        functools.partial(kernel, tiles, one, two, rows, cols, channels),
        out_shape=jax.ShapeDtypeStruct((rows, one, cols), BF16),
        in_specs=[pl.BlockSpec(memory_space=pltpu.SMEM)] + [vmem] * 9,
        out_specs=vmem,
        scratch_shapes=[
            pltpu.VMEM((rows + 2, 3 * one, LANES), BF16),
            pltpu.VMEM((rows // 2 + 2, 3 * one, LANES), BF16),
            pltpu.VMEM((rows // 2 + 2, 3 * two, LANES), BF16),
            pltpu.VMEM((rows + 2, 3 * (one + two), LANES), BF16),
            pltpu.VMEM((rows, one, LANES), F32),
            pltpu.VMEM((rows // 2, two, LANES), F32),
            pltpu.VMEM((rows // 2, one, LANES), F32),
            pltpu.VMEM((6, 2 * tiles, 2 * GROUPS, LANES), F32),
        ]
        + [pltpu.VMEM((5, width, LANES), BF16) for width in widths]
        + [pltpu.VMEM((6, width, LANES), BF16) for width in widths]
        + [pltpu.VMEM((width, LANES), BF16) for width in widths]
        + [
            pltpu.SemaphoreType.DMA((7, 7)),
            pltpu.SemaphoreType.DMA((7, 7)),
            pltpu.SemaphoreType.DMA((6,)),
            pltpu.SemaphoreType.DMA((6,)),
        ],
        compiler_params=pltpu.CompilerParams(
            collective_id=0, has_side_effects=True, vmem_limit_bytes=48 * 1024 * 1024),
    )(
        seam_codes, image, params,
        flat(kernel_upper_first, one), flat(kernel_upper_second, one),
        flat(kernel_lower_first, one), flat(kernel_lower_second, two),
        flat(kernel_decode_first, one + two), flat(kernel_decode_second, one), projection,
    )
    return jnp.transpose(result[:, :channels], (1, 0, 2))[None]


def solution(mesh):
    placed = (P("tile", None, "split", None),) + (P(),) * 16
    return jax.shard_map(
        per_device, mesh=mesh, in_specs=placed, out_specs=P("tile", None, "split", None), check_vma=False,
    )
```
